512 devices in a mesh: scen: 32 (over y, z_hi), tile: 16 (over x, z_lo, core).
Axes of the slice: x: 4, y: 8, z: 8 (z_hi: 4, z_lo: 2; z = z_hi * 2 + z_lo), core: 2. Of those that a mesh axis runs over, the one named last changes fastest.
Arguments:
- right_first: float32 [8192, 256], P('tile'), may hold values from -6 to 6
- right_scen: bfloat16 [32, 2048, 256], P('scen', 'tile'), may hold values from -6 to 6
- kkt_inverse: bfloat16 [32, 2048, 2048], P('scen', 'tile')
- border: bfloat16 [32, 2048, 8192], P('scen', None, 'tile'), may hold values from -0.09375 to 0.09375
- block_mask: int32 [32, 64], P('scen', 'tile'), may hold values 0 or 1
- factor_inverse: float32 [8192, 8192], P('scen', 'tile')
Outputs:
- first_sens: float32 [8192, 256], P('tile')
- scen_sens: float32 [32, 2048, 256], P('scen', 'tile')
The draws below stay inside these ranges and needn't reach their ends.
All inputs are finite; a program needn't handle non-finite values. No bound on the sum of `block_mask` on one device may be relied on, other than what follows from the above.
Results may differ from the reference program's by a relative error of at most 0.0045.
Values may be sent and summed in bfloat16 or wider, within the bound.
A program may use at most 64 MiB of HBM per device.

```python
import jax
import jax.numpy as jnp
from jax import lax

NS = 2048
N0 = 8192
DIRS = 256
SCENARIOS = 32
NBLK = 64


def draw_kkt_inverse(key, part):
    key = jax.random.fold_in(key, 11)
    first, second = jax.random.split(key)
    shape = (SCENARIOS, NS, NS)
    rows = lax.broadcasted_iota(jnp.int32, shape, 1)
    cols = lax.broadcasted_iota(jnp.int32, shape, 2)
    off = jax.random.normal(first, shape, jnp.float32) * (0.6 / jnp.sqrt(jnp.float32(NS)))
    diag = jax.random.uniform(second, shape, jnp.float32, 1.0, 2.0)
    return jnp.where(rows == cols, diag, off).astype(jnp.bfloat16)


def draw_factor_inverse(key, part):
    key = jax.random.fold_in(key, 23)
    first, second = jax.random.split(key)
    shape = (N0, N0)
    rows = lax.broadcasted_iota(jnp.int32, shape, 0)
    cols = lax.broadcasted_iota(jnp.int32, shape, 1)
    off = jax.random.normal(first, shape, jnp.float32) * (0.5 / jnp.sqrt(jnp.float32(N0)))
    diag = jax.random.uniform(second, shape, jnp.float32, 0.25, 0.5)
    return jnp.where(rows == cols, diag, jnp.where(rows > cols, off, 0.0))


def with_ends(values, key, smallest, largest):
    longest = values.shape.index(max(values.shape))
    spots = []
    for shift in (0, 1):
        where = [jax.random.randint(jax.random.fold_in(key, axis), (), 0, length) for axis, length in enumerate(values.shape)]
        where[longest] = (where[longest] + shift) % values.shape[longest]
        spots.append(tuple(where))
    return values.at[spots[0]].set(smallest).at[spots[1]].set(largest)


def shard_levels(own_key, dims, cuts, low, top_value):
    def one(position, parts):
        heights = jax.random.uniform(jax.random.fold_in(jax.random.fold_in(own_key, 6), position), (parts,), jnp.float32, low / len(cuts), top_value / len(cuts))
        return jnp.repeat(jnp.exp(heights), dims[position] // parts).reshape((-1,) + (1,) * (len(dims) - position - 1))

    loudness = one(*cuts[0])
    for cut in cuts[1:]:
        loudness = loudness * one(*cut)
    return loudness


def normal_values(rng, extent, scale, limit, cuts=(), dtype=jnp.bfloat16):
    result = jax.random.normal(rng, extent, jnp.float32) * scale
    if len(cuts) > 0:
        result = shard_levels(rng, extent, cuts, -0.22, 0.18) * result
    return jnp.clip(result, min=-limit, max=limit).astype(dtype)


def setup_inputs(seed: int = 0) -> dict:
    key_list = jax.random.split(jax.random.key(seed), 7)
    right_first = normal_values(key_list[0], (N0, DIRS), 1.0, 6.0, ((0, 16),), jnp.float32)
    right_scen = normal_values(key_list[1], (SCENARIOS, NS, DIRS), 1.0, 6.0, ((0, 32), (1, 16)))
    kkt_inverse = draw_kkt_inverse(jax.random.fold_in(key_list[6], 71), 0)
    border = normal_values(key_list[3], (SCENARIOS, NS, N0), (2 * NS) ** -0.5, 0.09375, ((0, 32), (2, 16)))
    block_mask = with_ends((jax.random.randint(key_list[4], (SCENARIOS, NBLK), 0, 5) < 3).astype(jnp.int32), jax.random.fold_in(key_list[4], 1), 0, 1)
    factor_inverse = draw_factor_inverse(jax.random.fold_in(key_list[6], 71), 0)
    return {"right_first": right_first, "right_scen": right_scen, "kkt_inverse": kkt_inverse, "border": border, "block_mask": block_mask, "factor_inverse": factor_inverse}


def reference(right_first, right_scen, kkt_inverse, border, block_mask, factor_inverse):
    width = border.shape[2] // block_mask.shape[1]
    expanded = jnp.repeat(block_mask.astype(jnp.bfloat16), width, axis=1)

    def forward(total, item):
        kinv, rights, edge, keep = item
        masked = edge * keep[None, :]
        weighted = jnp.dot(kinv, rights, preferred_element_type=jnp.float32).astype(jnp.bfloat16)
        return total + jnp.dot(masked.T, weighted, preferred_element_type=jnp.float32), None

    total, _ = lax.scan(forward, jnp.zeros(right_first.shape, jnp.float32), (kkt_inverse, right_scen, border, expanded))
    first_rhs = right_first - total
    half = jnp.dot(factor_inverse, first_rhs, precision=lax.Precision.HIGHEST)
    first_sens = jnp.dot(factor_inverse.T, half, precision=lax.Precision.HIGHEST)
    first_half = first_sens.astype(jnp.bfloat16)

    def backward(item):
        kinv, rights, edge, keep = item
        masked = edge * keep[None, :]
        images = jnp.dot(masked, first_half, preferred_element_type=jnp.float32)
        update = (rights.astype(jnp.float32) - images).astype(jnp.bfloat16)
        return jnp.dot(kinv, update, preferred_element_type=jnp.float32)

    scen_sens = lax.map(backward, (kkt_inverse, right_scen, border, expanded))
    return first_sens, scen_sens
```

```python
import jax
import jax.numpy as jnp
from jax import lax
from jax.experimental import pallas as pl
from jax.experimental.pallas import tpu as pltpu
from jax.sharding import PartitionSpec as P

MESH = pl.DeviceIdType.MESH
BF = jnp.bfloat16
F32 = jnp.float32
SCEN, TILE, CHIPS = 32, 16, 8
HALF = 128
Y_ORDER = (4, 3, 5, 2, 6, 1, 7, 0)
Z_ORDER = (2, 1, 3, 0)
SCEN_STEPS = [(dy, dz) for dy in Y_ORDER for dz in Z_ORDER if dy or dz]
CHIP_STEPS = [(2, 1), (1, 1), (3, 1), (2, 0), (1, 0), (3, 0), (0, 1)]


def kernel(
    rf, rs, kinv, bord, mask, fac,
    o1, o2,
    kc, bc, bt, fv, fhi, flo, fthi, ftlo, rfs, mx, mxs,
    ra, wb, pf, psend, cr, rh, hp, dr, hf, er, hh, hm, fs, fr, ug, sv, sr, o1v, o2v, hx,
    loc, ssem, rsem,
):
    s = lax.axis_index("scen")
    t = lax.axis_index("tile")
    q, c = t // 2, t % 2
    x, zl = q // 2, q % 2
    y, zh = s // 4, s % 4
    oc = 1 - c
    sib = (s, q * 2 + oc)

    def chip(dx, dz):
        return ((x + dx) % 4) * 2 + (zl + dz) % 2

    chips = [chip(dx, dz) for dx, dz in CHIP_STEPS]
    scens = [((y + dy) % 8) * 4 + (zh + dz) % 4 for dy, dz in SCEN_STEPS]

    def remote(src, dst, n, dev):
        pltpu.make_async_remote_copy(
            src_ref=src, dst_ref=dst, send_sem=ssem.at[n], recv_sem=rsem.at[n],
            device_id=dev, device_id_type=MESH,
        ).start()

    def arrived(ref, n):
        pltpu.make_async_copy(ref, ref, rsem.at[n]).wait()

    def sent(ref, n):
        pltpu.make_async_copy(ref, ref, ssem.at[n]).wait()

    def rows(i, n):
        return pl.ds(pl.multiple_of(i * n, n), n)

    own = [
        pltpu.make_async_copy(kinv.at[0], kc.at[rows(c, 128)], loc.at[0]),
        pltpu.make_async_copy(bord.at[0], bc.at[c], loc.at[1]),
        pltpu.make_async_copy(fac, fv.at[c], loc.at[2]),
        pltpu.make_async_copy(rf.at[rows(s % 16, 32), rows(c, 128)], rfs.at[c], loc.at[3]),
        pltpu.make_async_copy(rs.at[0, :, rows(c, 128)], ra.at[rows(t, 128)], loc.at[4]),
    ]
    for cp in own:
        cp.start()

    barrier = pltpu.get_barrier_semaphore()
    for p in chips:
        for cc in range(2):
            pl.semaphore_signal(barrier, inc=1, device_id=(s, p * 2 + cc), device_id_type=MESH)
    pl.semaphore_signal(barrier, inc=1, device_id=sib, device_id_type=MESH)
    for p in scens:
        pl.semaphore_signal(barrier, inc=1, device_id=(p, t), device_id_type=MESH)
    pl.semaphore_wait(barrier, TILE - 1 + SCEN - 1)

    for cc in range(2):
        for p in chips:
            remote(rs.at[0, :, rows(cc, 128)], ra.at[rows(t, 128)], 0, (s, p * 2 + cc))
    remote(rs.at[0, :, rows(oc, 128)], ra.at[rows(t, 128)], 0, sib)
    remote(kinv.at[0], kc.at[rows(c, 128)], 1, sib)
    remote(rf.at[rows(s % 16, 32), rows(oc, 128)], rfs.at[c], 2, sib)
    for b in range(4):
        mx[c, pl.ds(b * 8, 8)] = jnp.broadcast_to(mask[0:1, b : b + 1].astype(F32), (8, 128))
    remote(mx.at[c], mx.at[c], 3, sib)
    remote(bord.at[0], bc.at[c], 4, sib)
    remote(fac, fv.at[c], 5, sib)

    own[0].wait()
    own[4].wait()
    arrived(kc.at[rows(oc, 128)], 1)
    arrived(ra.at[pl.ds(0, 15 * 128)], 0)
    for i in range(2):
        r = pl.ds(i * 128, 128)
        w = jnp.dot(kc[r], ra[...], preferred_element_type=F32)
        wb[pl.ds(pl.multiple_of(q * 256 + i * 128, 128), 128)] = w.astype(BF)
    for p in chips:
        remote(wb.at[rows(q, 256)], wb.at[rows(q, 256)], 6, (s, p * 2 + c))

    own[1].wait()
    arrived(bc.at[oc], 4)
    arrived(mx.at[oc], 3)

    @pl.loop(0, 8)
    def _(i):
        for cc in range(2):
            for j in range(2):
                blk = bc[cc, rows(i, 256), pl.ds(j * 256, 256)]
                bt[pl.ds(cc * 512 + j * 256, 256), rows(i, 256)] = blk.T

    arrived(wb.at[pl.ds(0, 7 * 256)], 6)
    for k in range(4):
        r = (s // 8 + k) % 4
        p = jnp.dot(bt[rows(r, 256)], wb[...], preferred_element_type=F32)
        for j in range(2):
            keep = mx[r // 2, pl.ds(pl.multiple_of((r % 2) * 16 + j * 8, 8), 1)]
            v = jnp.where(keep > 0.5, p[j * 128 : (j + 1) * 128], 0.0)
            psend[pl.ds(r * 8 + j * 4, 4)] = v.astype(BF).reshape(4, 32, 128)
        for j in range(8):
            d = r * 8 + (s % 8 + j) % 8

            @pl.when(d != s)
            def _():
                remote(psend.at[d], cr.at[s], 7, (d, t))

    own[2].wait()
    arrived(fv.at[oc], 5)
    for cc in range(2):
        for j in range(2):
            v = fv[cc, :, pl.ds(j * 256, 256)]
            hi = v.astype(BF)
            lo = (v - hi.astype(F32)).astype(BF)
            at = pl.ds(cc * 512 + j * 256, 256)
            fhi[:, at] = hi
            flo[:, at] = lo
            fthi[at] = hi.T
            ftlo[at] = lo.T
    own[3].wait()
    arrived(rfs.at[oc], 2)
    cr[s] = psend[s]
    arrived(psend.at[pl.ds(0, 31)], 7)
    total = cr[0].astype(F32)
    for i in range(1, SCEN):
        total += cr[i].astype(F32)
    rh[rows(s, 32)] = (rfs[s // 16] - total).astype(BF)
    for p in scens:
        remote(rh.at[rows(s, 32)], rh.at[rows(s, 32)], 8, (p, t))
    arrived(rh.at[pl.ds(0, 31 * 32)], 8)

    for i in range(2):
        r = pl.ds(i * 128, 128)
        h = jnp.dot(fhi[r], rh[...], preferred_element_type=F32)
        h += jnp.dot(flo[r], rh[...], preferred_element_type=F32)
        hp[pl.ds(i * 4, 4)] = h.reshape(4, 32, 128)
    for p in chips:
        remote(hp.at[p], dr.at[q], 9, (s, p * 2 + c))
    dr[q] = hp[q]
    arrived(dr.at[pl.ds(0, 7)], 9)
    total = dr[0]
    for i in range(1, CHIPS):
        total += dr[i]
    hf[q] = total
    for p in chips:
        remote(hf.at[q], hf.at[q], 10, (s, p * 2 + c))
    arrived(hf.at[pl.ds(0, 7)], 10)

    half = hf[...].reshape(256, HALF)
    hhi = half.astype(BF)
    hlo = (half - hhi.astype(F32)).astype(BF)
    for k in range(4):
        r = (s // 8 + k) % 4
        v = jnp.dot(fthi[rows(r, 256)], hhi, preferred_element_type=F32)
        v += jnp.dot(fthi[rows(r, 256)], hlo, preferred_element_type=F32)
        v += jnp.dot(ftlo[rows(r, 256)], hhi, preferred_element_type=F32)
        pf[pl.ds(r * 8, 8)] = v.astype(BF).reshape(8, 32, 128)
        for j in range(8):
            d = r * 8 + (s % 8 + j) % 8

            @pl.when(d != s)
            def _():
                remote(pf.at[d], er.at[s], 11, (d, t))

    er[s] = pf[s]
    arrived(pf.at[pl.ds(0, 31)], 11)
    total = er[0].astype(F32)
    for i in range(1, SCEN):
        total += er[i].astype(F32)
    hh[rows(s, 32)] = total.astype(BF)
    for p in scens:
        remote(hh.at[rows(s, 32)], hh.at[rows(s, 32)], 12, (p, t))
    arrived(hh.at[pl.ds(0, 31 * 32)], 12)

    remote(hh.at[rows(oc, 512)], hx.at[pl.ds(0, 512)], 13, sib)
    for b in range(8):
        keep = mx[b // 4, pl.ds((b % 4) * 8, 1)]
        v = hh[pl.ds(b * 128, 128)].astype(F32)
        hm[pl.ds(b * 128, 128)] = jnp.where(keep > 0.5, v, 0.0).astype(BF)
    for p in [*chips, q]:
        at = rows(p, 256)
        v = jnp.dot(bc[0, at], hm[pl.ds(0, 512)], preferred_element_type=F32)
        v += jnp.dot(bc[1, at], hm[pl.ds(512, 512)], preferred_element_type=F32)
        fs[p] = v.astype(BF)
        if p is not q:
            remote(fs.at[p], fr.at[q], 14, (s, p * 2 + c))
    fr[q] = fs[q]

    arrived(hx, 13)
    o1v[:, rows(c, 128)] = hh[rows(c, 512)].astype(F32)
    o1v[:, rows(oc, 128)] = hx[...].astype(F32)
    out1 = pltpu.make_async_copy(o1v, o1, loc.at[5])
    out1.start()

    arrived(fs.at[pl.ds(0, 7)], 14)
    total = fr[0].astype(F32)
    for i in range(1, CHIPS):
        total += fr[i].astype(F32)
    ug[rows(q, 256)] = (ra[rows(q, 256)].astype(F32) - total).astype(BF)
    for p in chips:
        remote(ug.at[rows(q, 256)], ug.at[rows(q, 256)], 15, (s, p * 2 + c))
    arrived(ug.at[pl.ds(0, 7 * 256)], 15)
    sv[...] = jnp.dot(kc[rows(oc, 128)], ug[...], preferred_element_type=F32)
    remote(sv, sr, 16, sib)
    o2v[:, rows(c, 128)] = jnp.dot(kc[rows(c, 128)], ug[...], preferred_element_type=F32)
    arrived(sr, 16)
    o2v[:, rows(oc, 128)] = sr[...]
    out2 = pltpu.make_async_copy(o2v, o2.at[0], loc.at[6])
    out2.start()

    sent(ra.at[pl.ds(0, 15 * 128)], 0)
    sent(kc.at[rows(c, 128)], 1)
    sent(rfs.at[c], 2)
    sent(mx.at[c], 3)
    sent(bc.at[c], 4)
    sent(fv.at[c], 5)
    sent(wb.at[pl.ds(0, 7 * 256)], 6)
    sent(psend.at[pl.ds(0, 31)], 7)
    sent(rh.at[pl.ds(0, 31 * 32)], 8)
    sent(hp.at[pl.ds(0, 7)], 9)
    sent(hf.at[pl.ds(0, 7)], 10)
    sent(pf.at[pl.ds(0, 31)], 11)
    sent(hh.at[pl.ds(0, 31 * 32)], 12)
    sent(hx, 13)
    sent(fs.at[pl.ds(0, 7)], 14)
    sent(ug.at[pl.ds(0, 7 * 256)], 15)
    sent(sv, 16)
    out1.wait()
    out2.wait()


def per_device(right_first, right_scen, kkt_inverse, border, block_mask, factor_inverse):
    hbm = pl.BlockSpec(memory_space=pl.ANY)
    return pl.pallas_call(
        kernel,
        out_shape=(
            jax.ShapeDtypeStruct((512, 256), F32),
            jax.ShapeDtypeStruct((1, 128, 256), F32),
        ),
        in_specs=[hbm, hbm, hbm, hbm, pl.BlockSpec(memory_space=pltpu.VMEM), hbm],
        out_specs=(hbm, hbm),
        scratch_shapes=[
            pltpu.VMEM((256, 2048), BF),
            pltpu.VMEM((2, 2048, 512), BF),
            pltpu.VMEM((1024, 2048), BF),
            pltpu.VMEM((2, 256, 512), F32),
            pltpu.VMEM((256, 1024), BF),
            pltpu.VMEM((256, 1024), BF),
            pltpu.VMEM((1024, 256), BF),
            pltpu.VMEM((1024, 256), BF),
            pltpu.VMEM((2, 32, 128), F32),
            pltpu.VMEM((2, 32, 128), F32),
            pltpu.VMEM((8, 128), F32),
            pltpu.VMEM((2048, 128), BF),
            pltpu.VMEM((2048, 128), BF),
            pltpu.VMEM((32, 32, 128), BF),
            pltpu.VMEM((32, 32, 128), BF),
            pltpu.VMEM((32, 32, 128), BF),
            pltpu.VMEM((1024, 128), BF),
            pltpu.VMEM((8, 32, 128), F32),
            pltpu.VMEM((8, 32, 128), F32),
            pltpu.VMEM((8, 32, 128), F32),
            pltpu.VMEM((32, 32, 128), BF),
            pltpu.VMEM((1024, 128), BF),
            pltpu.VMEM((1024, 128), BF),
            pltpu.VMEM((8, 256, 128), BF),
            pltpu.VMEM((8, 256, 128), BF),
            pltpu.VMEM((2048, 128), BF),
            pltpu.VMEM((128, 128), F32),
            pltpu.VMEM((128, 128), F32),
            pltpu.VMEM((512, 256), F32),
            pltpu.VMEM((128, 256), F32),
            pltpu.VMEM((512, 128), BF),
            pltpu.SemaphoreType.DMA((7,)),
            pltpu.SemaphoreType.DMA((17,)),
            pltpu.SemaphoreType.DMA((17,)),
        ],
        compiler_params=pltpu.CompilerParams(
            collective_id=0, has_side_effects=True, vmem_limit_bytes=48 << 20
        ),
        cost_estimate=pl.CostEstimate(flops=3 * 10**9, bytes_accessed=8 << 20, transcendentals=0),
    )(right_first, right_scen, kkt_inverse, border, block_mask, factor_inverse)


def solution(mesh):
    in_specs = (
        P("tile", None),
        P("scen", "tile", None),
        P("scen", "tile", None),
        P("scen", None, "tile"),
        P("scen", "tile"),
        P("scen", "tile"),
    )
    out_specs = (P("tile", None), P("scen", "tile", None))
    return jax.shard_map(
        per_device, mesh=mesh, in_specs=in_specs, out_specs=out_specs, check_vma=False
    )
```

```python
import jax
import jax.numpy as jnp
from jax import lax
from jax.experimental import pallas as pl
from jax.experimental.pallas import tpu as pltpu
from jax.sharding import PartitionSpec as P

MESH = pl.DeviceIdType.MESH
BF = jnp.bfloat16
F32 = jnp.float32
SCEN, TILE, CHIPS = 32, 16, 8
HALF = 128
Y_ORDER = (4, 3, 5, 2, 6, 1, 7, 0)
Z_ORDER = (2, 1, 3, 0)
SCEN_STEPS = [(dy, dz) for dy in Y_ORDER for dz in Z_ORDER if dy or dz]
CHIP_STEPS = [(2, 1), (1, 1), (3, 1), (2, 0), (1, 0), (3, 0), (0, 1)]


def kernel(
    rf, rs, kinv, bord, mask, fac,
    o1, o2,
    kc, bc, bt, fv, fhi, flo, fthi, ftlo, rfs, mx,
    ra, wb, pf, psend, cr, rh, hp, dr, hf, er, hh, hm, fs, fr, ug, sv, o1v, o2v, hx,
    pacc, loc, ssem, rsem, ra_sem, wb_sem, rh_sem, ug_sem,
):
    s = lax.axis_index("scen")
    t = lax.axis_index("tile")
    q, c = t // 2, t % 2
    x, zl = q // 2, q % 2
    y, zh = s // 4, s % 4
    oc = 1 - c
    sib = (s, q * 2 + oc)

    def chip(dx, dz):
        return ((x + dx) % 4) * 2 + (zl + dz) % 2

    chips = [chip(dx, dz) for dx, dz in CHIP_STEPS]
    scens = [((y + dy) % 8) * 4 + (zh + dz) % 4 for dy, dz in SCEN_STEPS]

    def remote(src, dst, n, dev, landed=None):
        pltpu.make_async_remote_copy(
            src_ref=src, dst_ref=dst, send_sem=ssem.at[n],
            recv_sem=rsem.at[n] if landed is None else landed,
            device_id=dev, device_id_type=MESH,
        ).start()

    def arrived(ref, n):
        pltpu.make_async_copy(ref, ref, rsem.at[n]).wait()

    def landed(ref, sem):
        pltpu.make_async_copy(ref, ref, sem).wait()

    near = [q, *reversed(chips)]
    near_y = [(y + dy) % 8 for dy in reversed(Y_ORDER)]

    def sent(ref, n):
        pltpu.make_async_copy(ref, ref, ssem.at[n]).wait()

    def rows(i, n):
        return pl.ds(pl.multiple_of(i * n, n), n)

    own = [
        pltpu.make_async_copy(kinv.at[0], kc.at[rows(c, 128)], loc.at[0]),
        pltpu.make_async_copy(bord.at[0], bc.at[c], loc.at[1]),
        pltpu.make_async_copy(fac, fv.at[c], loc.at[2]),
        pltpu.make_async_copy(rf.at[rows(s % 16, 32), rows(c, 128)], rfs.at[c], loc.at[3]),
        pltpu.make_async_copy(rs.at[0, :, rows(c, 128)], ra.at[rows(t, 128)], loc.at[4]),
    ]
    for cp in own:
        cp.start()

    barrier = pltpu.get_barrier_semaphore()
    for p in chips:
        for cc in range(2):
            pl.semaphore_signal(barrier, inc=1, device_id=(s, p * 2 + cc), device_id_type=MESH)
    pl.semaphore_signal(barrier, inc=1, device_id=sib, device_id_type=MESH)
    for p in scens:
        pl.semaphore_signal(barrier, inc=1, device_id=(p, t), device_id_type=MESH)
    pl.semaphore_wait(barrier, TILE - 1 + SCEN - 1)

    for cc in (1, 0):
        for p in chips:
            remote(rs.at[0, :, rows(cc, 128)], ra.at[rows(t, 128)], 0, (s, p * 2 + cc), ra_sem.at[q])
    remote(rs.at[0, :, rows(oc, 128)], ra.at[rows(t, 128)], 0, sib, ra_sem.at[q])
    remote(kinv.at[0], kc.at[rows(c, 128)], 1, sib)
    remote(rf.at[rows(s % 16, 32), rows(oc, 128)], rfs.at[c], 2, sib)
    for b in range(4):
        mx[c, pl.ds(b * 8, 8)] = jnp.broadcast_to(mask[0:1, b : b + 1].astype(F32), (8, 128))
    remote(mx.at[c], mx.at[c], 3, sib)
    remote(bord.at[0], bc.at[c], 4, sib)
    remote(fac, fv.at[c], 5, sib)

    own[0].wait()
    own[4].wait()
    arrived(kc.at[rows(oc, 128)], 1)
    w = [jnp.zeros((128, HALF), F32)] * 2
    for p in near:
        landed(ra.at[rows(t, 128)] if p is q else ra.at[rows(p, 256)], ra_sem.at[p])
        for i in range(2):
            left = kc[pl.ds(i * 128, 128), rows(p, 256)]
            w[i] += jnp.dot(left, ra[rows(p, 256)], preferred_element_type=F32)
    for i in range(2):
        wb[pl.ds(pl.multiple_of(q * 256 + i * 128, 128), 128)] = w[i].astype(BF)
    for p in chips:
        remote(wb.at[rows(q, 256)], wb.at[rows(q, 256)], 6, (s, p * 2 + c), wb_sem.at[q])

    own[1].wait()
    arrived(bc.at[oc], 4)
    arrived(mx.at[oc], 3)

    @pl.loop(0, 8)
    def _(i):
        for cc in range(2):
            for j in range(2):
                blk = bc[cc, rows(i, 256), pl.ds(j * 256, 256)]
                bt[pl.ds(cc * 512 + j * 256, 256), rows(i, 256)] = blk.T

    for n, b in enumerate(near[:-1]):
        if b is not q:
            landed(wb.at[rows(b, 256)], wb_sem.at[b])

        @pl.loop(0, 4)
        def _(r):
            p = jnp.dot(bt[rows(r, 256), rows(b, 256)], wb[rows(b, 256)], preferred_element_type=F32)
            if n:
                p += pacc[rows(r, 256)]
            pacc[rows(r, 256)] = p

    b = near[-1]
    landed(wb.at[rows(b, 256)], wb_sem.at[b])
    for k in range(4):
        r = (s // 8 + k) % 4
        p = jnp.dot(bt[rows(r, 256), rows(b, 256)], wb[rows(b, 256)], preferred_element_type=F32)
        p += pacc[rows(r, 256)]
        for j in range(2):
            keep = mx[r // 2, pl.ds(pl.multiple_of((r % 2) * 16 + j * 8, 8), 1)]
            v = jnp.where(keep > 0.5, p[j * 128 : (j + 1) * 128], 0.0)
            psend[pl.ds(r * 8 + j * 4, 4)] = v.astype(BF).reshape(4, 32, 128)
        for j in range(8):
            d = r * 8 + (s % 8 + j) % 8

            @pl.when(d != s)
            def _():
                remote(psend.at[d], cr.at[s], 7, (d, t))

    own[2].wait()
    arrived(fv.at[oc], 5)
    for cc in range(2):
        for j in range(2):
            v = fv[cc, :, pl.ds(j * 256, 256)]
            hi = v.astype(BF)
            lo = (v - hi.astype(F32)).astype(BF)
            at = pl.ds(cc * 512 + j * 256, 256)
            fhi[:, at] = hi
            flo[:, at] = lo
            fthi[at] = hi.T
            ftlo[at] = lo.T
    own[3].wait()
    arrived(rfs.at[oc], 2)
    cr[s] = psend[s]
    arrived(psend.at[pl.ds(0, 31)], 7)
    total = cr[0].astype(F32)
    for i in range(1, SCEN):
        total += cr[i].astype(F32)
    rh[rows(s, 32)] = (rfs[s // 16] - total).astype(BF)
    for p in scens:
        remote(rh.at[rows(s, 32)], rh.at[rows(s, 32)], 8, (p, t), rh_sem.at[y])
    h = [jnp.zeros((128, HALF), F32)] * 2
    for n, p in enumerate(near_y):
        landed(rh.at[pl.ds(0, 128 if n else 96)], rh_sem.at[p])
        for i in range(2):
            r = pl.ds(i * 128, 128)
            for part in (fhi, flo):
                h[i] += jnp.dot(part[r, rows(p, 128)], rh[rows(p, 128)], preferred_element_type=F32)
    for i in range(2):
        hp[pl.ds(i * 4, 4)] = h[i].reshape(4, 32, 128)
    for p in chips:
        remote(hp.at[p], dr.at[q], 9, (s, p * 2 + c))
    dr[q] = hp[q]
    arrived(dr.at[pl.ds(0, 7)], 9)
    total = dr[0]
    for i in range(1, CHIPS):
        total += dr[i]
    hf[q] = total
    for p in chips:
        remote(hf.at[q], hf.at[q], 10, (s, p * 2 + c))
    arrived(hf.at[pl.ds(0, 7)], 10)

    half = hf[...].reshape(256, HALF)
    hhi = half.astype(BF)
    hlo = (half - hhi.astype(F32)).astype(BF)
    for k in range(4):
        r = (s // 8 + k) % 4
        v = jnp.dot(fthi[rows(r, 256)], hhi, preferred_element_type=F32)
        v += jnp.dot(fthi[rows(r, 256)], hlo, preferred_element_type=F32)
        v += jnp.dot(ftlo[rows(r, 256)], hhi, preferred_element_type=F32)
        pf[pl.ds(r * 8, 8)] = v.astype(BF).reshape(8, 32, 128)
        for j in range(8):
            d = r * 8 + (s % 8 + j) % 8

            @pl.when(d != s)
            def _():
                remote(pf.at[d], er.at[s], 11, (d, t))

    er[s] = pf[s]
    arrived(pf.at[pl.ds(0, 31)], 11)
    total = er[0].astype(F32)
    for i in range(1, SCEN):
        total += er[i].astype(F32)
    hh[rows(s, 32)] = total.astype(BF)
    for p in scens:
        remote(hh.at[rows(s, 32)], hh.at[rows(s, 32)], 12, (p, t))
    arrived(hh.at[pl.ds(0, 31 * 32)], 12)

    remote(hh.at[rows(oc, 512)], hx.at[pl.ds(0, 512)], 13, sib)
    for b in range(8):
        keep = mx[b // 4, pl.ds((b % 4) * 8, 1)]
        v = hh[pl.ds(b * 128, 128)].astype(F32)
        hm[pl.ds(b * 128, 128)] = jnp.where(keep > 0.5, v, 0.0).astype(BF)
    for p in [*chips, q]:
        at = rows(p, 256)
        v = jnp.dot(bc[0, at], hm[pl.ds(0, 512)], preferred_element_type=F32)
        v += jnp.dot(bc[1, at], hm[pl.ds(512, 512)], preferred_element_type=F32)
        fs[p] = v.astype(BF)
        if p is not q:
            remote(fs.at[p], fr.at[q], 14, (s, p * 2 + c))
    fr[q] = fs[q]

    arrived(hx, 13)
    o1v[:, rows(c, 128)] = hh[rows(c, 512)].astype(F32)
    o1v[:, rows(oc, 128)] = hx[...].astype(F32)
    out1 = pltpu.make_async_copy(o1v, o1, loc.at[5])
    out1.start()

    arrived(fs.at[pl.ds(0, 7)], 14)
    total = fr[0].astype(F32)
    for i in range(1, CHIPS):
        total += fr[i].astype(F32)
    ug[rows(q, 256)] = (ra[rows(q, 256)].astype(F32) - total).astype(BF)
    for p in chips:
        remote(ug.at[rows(q, 256)], ug.at[rows(q, 256)], 15, (s, p * 2 + c), ug_sem.at[q])
    v = [jnp.zeros((128, HALF), F32)] * 2
    for p in near:
        if p is not q:
            landed(ug.at[rows(p, 256)], ug_sem.at[p])
        for i, cc in enumerate((oc, c)):
            left = kc[rows(cc, 128), rows(p, 256)]
            v[i] += jnp.dot(left, ug[rows(p, 256)], preferred_element_type=F32)
    sv[...] = v[0]
    remote(sv, o2.at[0, :, rows(c, 128)], 16, sib)
    o2v[...] = v[1]
    out2 = pltpu.make_async_copy(o2v, o2.at[0, :, rows(c, 128)], loc.at[6])
    out2.start()
    arrived(sv, 16)

    sent(ra.at[pl.ds(0, 15 * 128)], 0)
    sent(kc.at[rows(c, 128)], 1)
    sent(rfs.at[c], 2)
    sent(mx.at[c], 3)
    sent(bc.at[c], 4)
    sent(fv.at[c], 5)
    sent(wb.at[pl.ds(0, 7 * 256)], 6)
    sent(psend.at[pl.ds(0, 31)], 7)
    sent(rh.at[pl.ds(0, 31 * 32)], 8)
    sent(hp.at[pl.ds(0, 7)], 9)
    sent(hf.at[pl.ds(0, 7)], 10)
    sent(pf.at[pl.ds(0, 31)], 11)
    sent(hh.at[pl.ds(0, 31 * 32)], 12)
    sent(hx, 13)
    sent(fs.at[pl.ds(0, 7)], 14)
    sent(ug.at[pl.ds(0, 7 * 256)], 15)
    sent(sv, 16)
    out1.wait()
    out2.wait()


def per_device(right_first, right_scen, kkt_inverse, border, block_mask, factor_inverse):
    hbm = pl.BlockSpec(memory_space=pl.ANY)
    return pl.pallas_call(
        kernel,
        out_shape=(
            jax.ShapeDtypeStruct((512, 256), F32),
            jax.ShapeDtypeStruct((1, 128, 256), F32),
        ),
        in_specs=[hbm, hbm, hbm, hbm, pl.BlockSpec(memory_space=pltpu.VMEM), hbm],
        out_specs=(hbm, hbm),
        scratch_shapes=[
            pltpu.VMEM((256, 2048), BF),
            pltpu.VMEM((2, 2048, 512), BF),
            pltpu.VMEM((1024, 2048), BF),
            pltpu.VMEM((2, 256, 512), F32),
            pltpu.VMEM((256, 1024), BF),
            pltpu.VMEM((256, 1024), BF),
            pltpu.VMEM((1024, 256), BF),
            pltpu.VMEM((1024, 256), BF),
            pltpu.VMEM((2, 32, 128), F32),
            pltpu.VMEM((2, 32, 128), F32),
            pltpu.VMEM((2048, 128), BF),
            pltpu.VMEM((2048, 128), BF),
            pltpu.VMEM((32, 32, 128), BF),
            pltpu.VMEM((32, 32, 128), BF),
            pltpu.VMEM((32, 32, 128), BF),
            pltpu.VMEM((1024, 128), BF),
            pltpu.VMEM((8, 32, 128), F32),
            pltpu.VMEM((8, 32, 128), F32),
            pltpu.VMEM((8, 32, 128), F32),
            pltpu.VMEM((32, 32, 128), BF),
            pltpu.VMEM((1024, 128), BF),
            pltpu.VMEM((1024, 128), BF),
            pltpu.VMEM((8, 256, 128), BF),
            pltpu.VMEM((8, 256, 128), BF),
            pltpu.VMEM((2048, 128), BF),
            pltpu.VMEM((128, 128), F32),
            pltpu.VMEM((512, 256), F32),
            pltpu.VMEM((128, 128), F32),
            pltpu.VMEM((512, 128), BF),
            pltpu.VMEM((1024, 128), F32),
            pltpu.SemaphoreType.DMA((7,)),
            pltpu.SemaphoreType.DMA((17,)),
            pltpu.SemaphoreType.DMA((17,)),
            *[pltpu.SemaphoreType.DMA((8,))] * 4,
        ],
        compiler_params=pltpu.CompilerParams(
            collective_id=0, has_side_effects=True, vmem_limit_bytes=62 << 20
        ),
        cost_estimate=pl.CostEstimate(flops=3 * 10**9, bytes_accessed=8 << 20, transcendentals=0),
    )(right_first, right_scen, kkt_inverse, border, block_mask, factor_inverse)


def solution(mesh):
    in_specs = (
        P("tile", None),
        P("scen", "tile", None),
        P("scen", "tile", None),
        P("scen", None, "tile"),
        P("scen", "tile"),
        P("scen", "tile"),
    )
    out_specs = (P("tile", None), P("scen", "tile", None))
    return jax.shard_map(
        per_device, mesh=mesh, in_specs=in_specs, out_specs=out_specs, check_vma=False
    )
```

```python
import jax
import jax.numpy as jnp
from jax import lax
from jax.experimental import pallas as pl
from jax.experimental.pallas import tpu as pltpu
from jax.sharding import PartitionSpec as P

MESH = pl.DeviceIdType.MESH
BF = jnp.bfloat16
F32 = jnp.float32
SCEN, TILE, CHIPS = 32, 16, 8
HALF = 128
Y_ORDER = (4, 3, 5, 2, 6, 1, 7, 0)
Z_ORDER = (2, 1, 3, 0)
SCEN_STEPS = [(dy, dz) for dy in Y_ORDER for dz in Z_ORDER if dy or dz]
CHIP_STEPS = [(2, 1), (1, 1), (3, 1), (2, 0), (1, 0), (3, 0), (0, 1)]


def kernel(
    rf, rs, kinv, bord, mask, fac,
    o1, o2,
    kc, bc, bt, fv, fhi, flo, fthi, ftlo, rfs, mx,
    ra, wb, pf, psend, cr, rh, hp, dr, hf, er, hh, hm, fs, fr, ug, sv, o1v, o2v, hx,
    loc, ssem, rsem,
):
    s = lax.axis_index("scen")
    t = lax.axis_index("tile")
    q, c = t // 2, t % 2
    x, zl = q // 2, q % 2
    y, zh = s // 4, s % 4
    oc = 1 - c
    sib = (s, q * 2 + oc)

    def chip(dx, dz):
        return ((x + dx) % 4) * 2 + (zl + dz) % 2

    chips = [chip(dx, dz) for dx, dz in CHIP_STEPS]
    scens = [((y + dy) % 8) * 4 + (zh + dz) % 4 for dy, dz in SCEN_STEPS]

    def remote(src, dst, n, dev):
        pltpu.make_async_remote_copy(
            src_ref=src, dst_ref=dst, send_sem=ssem.at[n], recv_sem=rsem.at[n],
            device_id=dev, device_id_type=MESH,
        ).start()

    def arrived(ref, n):
        pltpu.make_async_copy(ref, ref, rsem.at[n]).wait()

    def sent(ref, n):
        pltpu.make_async_copy(ref, ref, ssem.at[n]).wait()

    def rows(i, n):
        return pl.ds(pl.multiple_of(i * n, n), n)

    own = [
        pltpu.make_async_copy(kinv.at[0], kc.at[rows(c, 128)], loc.at[0]),
        pltpu.make_async_copy(bord.at[0], bc.at[c], loc.at[1]),
        pltpu.make_async_copy(fac, fv.at[c], loc.at[2]),
        pltpu.make_async_copy(rf.at[rows(s % 16, 32), rows(c, 128)], rfs.at[c], loc.at[3]),
        pltpu.make_async_copy(rs.at[0, :, rows(c, 128)], ra.at[rows(t, 128)], loc.at[4]),
    ]
    for cp in own:
        cp.start()

    barrier = pltpu.get_barrier_semaphore()
    for p in chips:
        for cc in range(2):
            pl.semaphore_signal(barrier, inc=1, device_id=(s, p * 2 + cc), device_id_type=MESH)
    pl.semaphore_signal(barrier, inc=1, device_id=sib, device_id_type=MESH)
    for p in scens:
        pl.semaphore_signal(barrier, inc=1, device_id=(p, t), device_id_type=MESH)
    pl.semaphore_wait(barrier, TILE - 1 + SCEN - 1)

    for cc in (1, 0):
        for p in chips:
            remote(rs.at[0, :, rows(cc, 128)], ra.at[rows(t, 128)], 0, (s, p * 2 + cc))
    remote(rs.at[0, :, rows(oc, 128)], ra.at[rows(t, 128)], 0, sib)
    remote(kinv.at[0], kc.at[rows(c, 128)], 1, sib)
    remote(rf.at[rows(s % 16, 32), rows(oc, 128)], rfs.at[c], 2, sib)
    for b in range(4):
        mx[c, pl.ds(b * 8, 8)] = jnp.broadcast_to(mask[0:1, b : b + 1].astype(F32), (8, 128))
    remote(mx.at[c], mx.at[c], 3, sib)
    remote(bord.at[0], bc.at[c], 4, sib)
    remote(fac, fv.at[c], 5, sib)

    own[0].wait()
    own[4].wait()
    arrived(kc.at[rows(oc, 128)], 1)
    arrived(ra.at[pl.ds(0, 15 * 128)], 0)
    for i in range(2):
        r = pl.ds(i * 128, 128)
        w = jnp.dot(kc[r], ra[...], preferred_element_type=F32)
        wb[pl.ds(pl.multiple_of(q * 256 + i * 128, 128), 128)] = w.astype(BF)
    for p in chips:
        remote(wb.at[rows(q, 256)], wb.at[rows(q, 256)], 6, (s, p * 2 + c))

    own[1].wait()
    arrived(bc.at[oc], 4)
    arrived(mx.at[oc], 3)

    @pl.loop(0, 8)
    def _(i):
        for cc in range(2):
            for j in range(2):
                blk = bc[cc, rows(i, 256), pl.ds(j * 256, 256)]
                bt[pl.ds(cc * 512 + j * 256, 256), rows(i, 256)] = blk.T

    arrived(wb.at[pl.ds(0, 7 * 256)], 6)
    for k in range(4):
        r = (s // 8 + k) % 4
        p = jnp.dot(bt[rows(r, 256)], wb[...], preferred_element_type=F32)
        for j in range(2):
            keep = mx[r // 2, pl.ds(pl.multiple_of((r % 2) * 16 + j * 8, 8), 1)]
            v = jnp.where(keep > 0.5, p[j * 128 : (j + 1) * 128], 0.0)
            psend[pl.ds(r * 8 + j * 4, 4)] = v.astype(BF).reshape(4, 32, 128)
        for j in range(8):
            d = r * 8 + (s % 8 + j) % 8

            @pl.when(d != s)
            def _():
                remote(psend.at[d], cr.at[s], 7, (d, t))

    own[2].wait()
    arrived(fv.at[oc], 5)
    for cc in range(2):
        for j in range(2):
            v = fv[cc, :, pl.ds(j * 256, 256)]
            hi = v.astype(BF)
            lo = (v - hi.astype(F32)).astype(BF)
            at = pl.ds(cc * 512 + j * 256, 256)
            fhi[:, at] = hi
            flo[:, at] = lo
            fthi[at] = hi.T
            ftlo[at] = lo.T
    own[3].wait()
    arrived(rfs.at[oc], 2)
    cr[s] = psend[s]
    arrived(psend.at[pl.ds(0, 31)], 7)
    total = cr[0].astype(F32)
    for i in range(1, SCEN):
        total += cr[i].astype(F32)
    rh[rows(s, 32)] = (rfs[s // 16] - total).astype(BF)
    for p in scens:
        remote(rh.at[rows(s, 32)], rh.at[rows(s, 32)], 8, (p, t))
    arrived(rh.at[pl.ds(0, 31 * 32)], 8)

    for i in range(2):
        r = pl.ds(i * 128, 128)
        h = jnp.dot(fhi[r], rh[...], preferred_element_type=F32)
        h += jnp.dot(flo[r], rh[...], preferred_element_type=F32)
        hp[pl.ds(i * 4, 4)] = h.reshape(4, 32, 128)
    for p in chips:
        remote(hp.at[p], dr.at[q], 9, (s, p * 2 + c))
    dr[q] = hp[q]
    arrived(dr.at[pl.ds(0, 7)], 9)
    total = dr[0]
    for i in range(1, CHIPS):
        total += dr[i]
    hf[q] = total
    for p in chips:
        remote(hf.at[q], hf.at[q], 10, (s, p * 2 + c))
    arrived(hf.at[pl.ds(0, 7)], 10)

    half = hf[...].reshape(256, HALF)
    hhi = half.astype(BF)
    hlo = (half - hhi.astype(F32)).astype(BF)
    for k in range(4):
        r = (s // 8 + k) % 4
        v = jnp.dot(fthi[rows(r, 256)], hhi, preferred_element_type=F32)
        v += jnp.dot(fthi[rows(r, 256)], hlo, preferred_element_type=F32)
        v += jnp.dot(ftlo[rows(r, 256)], hhi, preferred_element_type=F32)
        pf[pl.ds(r * 8, 8)] = v.astype(BF).reshape(8, 32, 128)
        for j in range(8):
            d = r * 8 + (s % 8 + j) % 8

            @pl.when(d != s)
            def _():
                remote(pf.at[d], er.at[s], 11, (d, t))

    er[s] = pf[s]
    arrived(pf.at[pl.ds(0, 31)], 11)
    total = er[0].astype(F32)
    for i in range(1, SCEN):
        total += er[i].astype(F32)
    hh[rows(s, 32)] = total.astype(BF)
    for p in scens:
        remote(hh.at[rows(s, 32)], hh.at[rows(s, 32)], 12, (p, t))
    arrived(hh.at[pl.ds(0, 31 * 32)], 12)

    remote(hh.at[rows(oc, 512)], hx.at[pl.ds(0, 512)], 13, sib)
    for b in range(8):
        keep = mx[b // 4, pl.ds((b % 4) * 8, 1)]
        v = hh[pl.ds(b * 128, 128)].astype(F32)
        hm[pl.ds(b * 128, 128)] = jnp.where(keep > 0.5, v, 0.0).astype(BF)
    for p in [*chips, q]:
        at = rows(p, 256)
        v = jnp.dot(bc[0, at], hm[pl.ds(0, 512)], preferred_element_type=F32)
        v += jnp.dot(bc[1, at], hm[pl.ds(512, 512)], preferred_element_type=F32)
        fs[p] = v.astype(BF)
        if p is not q:
            remote(fs.at[p], fr.at[q], 14, (s, p * 2 + c))
    fr[q] = fs[q]

    arrived(hx, 13)
    o1v[:, rows(c, 128)] = hh[rows(c, 512)].astype(F32)
    o1v[:, rows(oc, 128)] = hx[...].astype(F32)
    out1 = pltpu.make_async_copy(o1v, o1, loc.at[5])
    out1.start()

    arrived(fs.at[pl.ds(0, 7)], 14)
    total = fr[0].astype(F32)
    for i in range(1, CHIPS):
        total += fr[i].astype(F32)
    ug[rows(q, 256)] = (ra[rows(q, 256)].astype(F32) - total).astype(BF)
    for p in chips:
        remote(ug.at[rows(q, 256)], ug.at[rows(q, 256)], 15, (s, p * 2 + c))
    arrived(ug.at[pl.ds(0, 7 * 256)], 15)
    sv[...] = jnp.dot(kc[rows(oc, 128)], ug[...], preferred_element_type=F32)
    remote(sv, o2.at[0, :, rows(c, 128)], 16, sib)
    o2v[...] = jnp.dot(kc[rows(c, 128)], ug[...], preferred_element_type=F32)
    out2 = pltpu.make_async_copy(o2v, o2.at[0, :, rows(c, 128)], loc.at[6])
    out2.start()
    arrived(sv, 16)

    sent(ra.at[pl.ds(0, 15 * 128)], 0)
    sent(kc.at[rows(c, 128)], 1)
    sent(rfs.at[c], 2)
    sent(mx.at[c], 3)
    sent(bc.at[c], 4)
    sent(fv.at[c], 5)
    sent(wb.at[pl.ds(0, 7 * 256)], 6)
    sent(psend.at[pl.ds(0, 31)], 7)
    sent(rh.at[pl.ds(0, 31 * 32)], 8)
    sent(hp.at[pl.ds(0, 7)], 9)
    sent(hf.at[pl.ds(0, 7)], 10)
    sent(pf.at[pl.ds(0, 31)], 11)
    sent(hh.at[pl.ds(0, 31 * 32)], 12)
    sent(hx, 13)
    sent(fs.at[pl.ds(0, 7)], 14)
    sent(ug.at[pl.ds(0, 7 * 256)], 15)
    sent(sv, 16)
    out1.wait()
    out2.wait()


def per_device(right_first, right_scen, kkt_inverse, border, block_mask, factor_inverse):
    hbm = pl.BlockSpec(memory_space=pl.ANY)
    return pl.pallas_call(
        kernel,
        out_shape=(
            jax.ShapeDtypeStruct((512, 256), F32),
            jax.ShapeDtypeStruct((1, 128, 256), F32),
        ),
        in_specs=[hbm, hbm, hbm, hbm, pl.BlockSpec(memory_space=pltpu.VMEM), hbm],
        out_specs=(hbm, hbm),
        scratch_shapes=[
            pltpu.VMEM((256, 2048), BF),
            pltpu.VMEM((2, 2048, 512), BF),
            pltpu.VMEM((1024, 2048), BF),
            pltpu.VMEM((2, 256, 512), F32),
            pltpu.VMEM((256, 1024), BF),
            pltpu.VMEM((256, 1024), BF),
            pltpu.VMEM((1024, 256), BF),
            pltpu.VMEM((1024, 256), BF),
            pltpu.VMEM((2, 32, 128), F32),
            pltpu.VMEM((2, 32, 128), F32),
            pltpu.VMEM((2048, 128), BF),
            pltpu.VMEM((2048, 128), BF),
            pltpu.VMEM((32, 32, 128), BF),
            pltpu.VMEM((32, 32, 128), BF),
            pltpu.VMEM((32, 32, 128), BF),
            pltpu.VMEM((1024, 128), BF),
            pltpu.VMEM((8, 32, 128), F32),
            pltpu.VMEM((8, 32, 128), F32),
            pltpu.VMEM((8, 32, 128), F32),
            pltpu.VMEM((32, 32, 128), BF),
            pltpu.VMEM((1024, 128), BF),
            pltpu.VMEM((1024, 128), BF),
            pltpu.VMEM((8, 256, 128), BF),
            pltpu.VMEM((8, 256, 128), BF),
            pltpu.VMEM((2048, 128), BF),
            pltpu.VMEM((128, 128), F32),
            pltpu.VMEM((512, 256), F32),
            pltpu.VMEM((128, 128), F32),
            pltpu.VMEM((512, 128), BF),
            pltpu.SemaphoreType.DMA((7,)),
            pltpu.SemaphoreType.DMA((17,)),
            pltpu.SemaphoreType.DMA((17,)),
        ],
        compiler_params=pltpu.CompilerParams(
            collective_id=0, has_side_effects=True, vmem_limit_bytes=53 << 20
        ),
        cost_estimate=pl.CostEstimate(flops=3 * 10**9, bytes_accessed=8 << 20, transcendentals=0),
    )(right_first, right_scen, kkt_inverse, border, block_mask, factor_inverse)


def solution(mesh):
    in_specs = (
        P("tile", None),
        P("scen", "tile", None),
        P("scen", "tile", None),
        P("scen", None, "tile"),
        P("scen", "tile"),
        P("scen", "tile"),
    )
    out_specs = (P("tile", None), P("scen", "tile", None))
    return jax.shard_map(
        per_device, mesh=mesh, in_specs=in_specs, out_specs=out_specs, check_vma=False
    )
```

```python
import jax
import jax.numpy as jnp
from jax import lax
from jax.experimental import pallas as pl
from jax.experimental.pallas import tpu as pltpu
from jax.sharding import PartitionSpec as P

MESH = pl.DeviceIdType.MESH
BF = jnp.bfloat16
F32 = jnp.float32
SCEN, TILE, CHIPS = 32, 16, 8
HALF = 128
Y_ORDER = (4, 3, 5, 2, 6, 1, 7, 0)
Z_ORDER = (2, 1, 3, 0)
SCEN_STEPS = [(dy, dz) for dy in Y_ORDER for dz in Z_ORDER if dy or dz]
CHIP_STEPS = [(2, 1), (1, 1), (3, 1), (2, 0), (1, 0), (3, 0), (0, 1)]


def kernel(
    rf, rs, kinv, bord, mask, fac,
    o1, o2,
    kc, bc, bt, fv, fhi, flo, fthi, ftlo, rfs, mx,
    ra, r2, wb, pf, psend, cr, rh, hp, dr, hf, er, hh, hm, fs, fr, ug, sv, o1v, o2v, hx,
    loc, ssem, rsem,
):
    s = lax.axis_index("scen")
    t = lax.axis_index("tile")
    q, c = t // 2, t % 2
    x, zl = q // 2, q % 2
    y, zh = s // 4, s % 4
    oc = 1 - c
    sib = (s, q * 2 + oc)

    def chip(dx, dz):
        return ((x + dx) % 4) * 2 + (zl + dz) % 2

    chips = [chip(dx, dz) for dx, dz in CHIP_STEPS]
    scens = [((y + dy) % 8) * 4 + (zh + dz) % 4 for dy, dz in SCEN_STEPS]

    def remote(src, dst, n, dev):
        pltpu.make_async_remote_copy(
            src_ref=src, dst_ref=dst, send_sem=ssem.at[n], recv_sem=rsem.at[n],
            device_id=dev, device_id_type=MESH,
        ).start()

    def arrived(ref, n):
        pltpu.make_async_copy(ref, ref, rsem.at[n]).wait()

    def sent(ref, n):
        pltpu.make_async_copy(ref, ref, ssem.at[n]).wait()

    def rows(i, n):
        return pl.ds(pl.multiple_of(i * n, n), n)

    own = [
        pltpu.make_async_copy(kinv.at[0], kc.at[rows(c, 128)], loc.at[0]),
        pltpu.make_async_copy(bord.at[0], bc.at[c], loc.at[1]),
        pltpu.make_async_copy(fac, fv.at[c], loc.at[2]),
        pltpu.make_async_copy(rf.at[rows(s % 16, 32), rows(c, 128)], rfs.at[c], loc.at[3]),
        pltpu.make_async_copy(rs.at[0, :, rows(c, 128)], ra.at[rows(t, 128)], loc.at[4]),
        pltpu.make_async_copy(rs.at[0, :, rows(oc, 128)], r2.at[rows(c, 128)], loc.at[7]),
    ]
    for cp in own:
        cp.start()

    barrier = pltpu.get_barrier_semaphore()
    for p in chips:
        for cc in range(2):
            pl.semaphore_signal(barrier, inc=1, device_id=(s, p * 2 + cc), device_id_type=MESH)
    pl.semaphore_signal(barrier, inc=1, device_id=sib, device_id_type=MESH)
    for p in scens:
        pl.semaphore_signal(barrier, inc=1, device_id=(p, t), device_id_type=MESH)
    pl.semaphore_wait(barrier, TILE - 1 + SCEN - 1)

    for cc in (1, 0):
        for p in chips:
            remote(rs.at[0, :, rows(cc, 128)], ra.at[rows(t, 128)], 0, (s, p * 2 + cc))
    remote(rs.at[0, :, rows(oc, 128)], ra.at[rows(t, 128)], 0, sib)
    remote(kinv.at[0], kc.at[rows(c, 128)], 1, sib)
    remote(rf.at[rows(s % 16, 32), rows(oc, 128)], rfs.at[c], 2, sib)
    for b in range(4):
        mx[c, pl.ds(b * 8, 8)] = jnp.broadcast_to(mask[0:1, b : b + 1].astype(F32), (8, 128))
    remote(mx.at[c], mx.at[c], 3, sib)
    remote(bord.at[0], bc.at[c], 4, sib)
    remote(fac, fv.at[c], 5, sib)
    remote(rs.at[0, :, rows(c, 128)], r2.at[rows(c, 128)], 17, sib)

    own[0].wait()
    own[4].wait()
    arrived(kc.at[rows(oc, 128)], 1)
    arrived(ra.at[pl.ds(0, 15 * 128)], 0)
    for i in range(2):
        r = pl.ds(i * 128, 128)
        w = jnp.dot(kc[r], ra[...], preferred_element_type=F32)
        wb[pl.ds(pl.multiple_of(q * 256 + i * 128, 128), 128)] = w.astype(BF)
    for p in chips:
        remote(wb.at[rows(q, 256)], wb.at[rows(q, 256)], 6, (s, p * 2 + c))

    own[1].wait()
    arrived(bc.at[oc], 4)
    arrived(mx.at[oc], 3)

    @pl.loop(0, 8)
    def _(i):
        for cc in range(2):
            for j in range(2):
                blk = bc[cc, rows(i, 256), pl.ds(j * 256, 256)]
                bt[pl.ds(cc * 512 + j * 256, 256), rows(i, 256)] = blk.T

    arrived(wb.at[pl.ds(0, 7 * 256)], 6)
    for k in range(4):
        r = (s // 8 + k) % 4
        p = jnp.dot(bt[rows(r, 256)], wb[...], preferred_element_type=F32)
        for j in range(2):
            keep = mx[r // 2, pl.ds(pl.multiple_of((r % 2) * 16 + j * 8, 8), 1)]
            v = jnp.where(keep > 0.5, p[j * 128 : (j + 1) * 128], 0.0)
            psend[pl.ds(r * 8 + j * 4, 4)] = v.astype(BF).reshape(4, 32, 128)
        for j in range(8):
            d = r * 8 + (s % 8 + j) % 8

            @pl.when(d != s)
            def _():
                remote(psend.at[d], cr.at[s], 7, (d, t))

    own[2].wait()
    arrived(fv.at[oc], 5)
    for cc in range(2):
        for j in range(2):
            v = fv[cc, :, pl.ds(j * 256, 256)]
            hi = v.astype(BF)
            lo = (v - hi.astype(F32)).astype(BF)
            at = pl.ds(cc * 512 + j * 256, 256)
            fhi[:, at] = hi
            flo[:, at] = lo
            fthi[at] = hi.T
            ftlo[at] = lo.T
    own[3].wait()
    arrived(rfs.at[oc], 2)
    own[5].wait()
    arrived(r2.at[rows(oc, 128)], 17)
    cr[s] = psend[s]
    arrived(psend.at[pl.ds(0, 31)], 7)
    total = cr[0].astype(F32)
    for i in range(1, SCEN):
        total += cr[i].astype(F32)
    rh[rows(s, 32)] = (rfs[s // 16] - total).astype(BF)
    for p in scens:
        remote(rh.at[rows(s, 32)], rh.at[rows(s, 32)], 8, (p, t))
    arrived(rh.at[pl.ds(0, 31 * 32)], 8)

    for i in range(2):
        r = pl.ds(i * 128, 128)
        h = jnp.dot(fhi[r], rh[...], preferred_element_type=F32)
        h += jnp.dot(flo[r], rh[...], preferred_element_type=F32)
        hp[pl.ds(i * 4, 4)] = h.reshape(4, 32, 128)
    for p in chips:
        remote(hp.at[p], dr.at[q], 9, (s, p * 2 + oc))
    remote(hp.at[q], dr.at[q], 9, sib)
    arrived(dr, 9)
    total = dr[0]
    for i in range(1, CHIPS):
        total += dr[i]
    hf[q] = total
    for p in chips:
        remote(hf.at[q], hf.at[q], 10, (s, p * 2 + c))
    arrived(hf.at[pl.ds(0, 7)], 10)

    half = hf[...].reshape(256, HALF)
    hhi = half.astype(BF)
    hlo = (half - hhi.astype(F32)).astype(BF)
    for k in range(4):
        r = (s // 8 + k) % 4
        v = jnp.dot(fthi[rows(r, 256)], hhi, preferred_element_type=F32)
        v += jnp.dot(fthi[rows(r, 256)], hlo, preferred_element_type=F32)
        v += jnp.dot(ftlo[rows(r, 256)], hhi, preferred_element_type=F32)
        pf[pl.ds(r * 8, 8)] = v.astype(BF).reshape(8, 32, 128)
        for j in range(8):
            d = r * 8 + (s % 8 + j) % 8

            @pl.when(d != s)
            def _():
                remote(pf.at[d], er.at[s], 11, (d, t))

    er[s] = pf[s]
    arrived(pf.at[pl.ds(0, 31)], 11)
    total = er[0].astype(F32)
    for i in range(1, SCEN):
        total += er[i].astype(F32)
    hh[rows(s, 32)] = total.astype(BF)
    for p in scens:
        remote(hh.at[rows(s, 32)], hh.at[rows(s, 32)], 12, (p, t))
    arrived(hh.at[pl.ds(0, 31 * 32)], 12)

    remote(hh.at[rows(oc, 512)], hx.at[pl.ds(0, 512)], 13, sib)
    for b in range(8):
        keep = mx[b // 4, pl.ds((b % 4) * 8, 1)]
        v = hh[pl.ds(b * 128, 128)].astype(F32)
        hm[pl.ds(b * 128, 128)] = jnp.where(keep > 0.5, v, 0.0).astype(BF)
    for p in [*chips, q]:
        at = rows(p, 256)
        v = jnp.dot(bc[0, at], hm[pl.ds(0, 512)], preferred_element_type=F32)
        v += jnp.dot(bc[1, at], hm[pl.ds(512, 512)], preferred_element_type=F32)
        fs[p] = v.astype(BF)
        if p is not q:
            remote(fs.at[p], fr.at[q], 14, (s, p * 2 + c))
    fr[q] = fs[q]

    arrived(hx, 13)
    o1v[:, rows(oc, 128)] = hh[rows(c, 512)].astype(F32)
    o1v[:, rows(c, 128)] = hx[...].astype(F32)
    out1 = pltpu.make_async_copy(o1v, o1, loc.at[5])
    out1.start()

    arrived(fs.at[pl.ds(0, 7)], 14)
    total = fr[0].astype(F32)
    for i in range(1, CHIPS):
        total += fr[i].astype(F32)
    ug[rows(q, 256)] = (r2[...].astype(F32) - total).astype(BF)
    for p in chips:
        remote(ug.at[rows(q, 256)], ug.at[rows(q, 256)], 15, (s, p * 2 + c))
    arrived(ug.at[pl.ds(0, 7 * 256)], 15)
    sv[...] = jnp.dot(kc[rows(oc, 128)], ug[...], preferred_element_type=F32)
    remote(sv, o2.at[0, :, rows(oc, 128)], 16, sib)
    o2v[...] = jnp.dot(kc[rows(c, 128)], ug[...], preferred_element_type=F32)
    out2 = pltpu.make_async_copy(o2v, o2.at[0, :, rows(oc, 128)], loc.at[6])
    out2.start()
    arrived(sv, 16)

    sent(ra.at[pl.ds(0, 15 * 128)], 0)
    sent(kc.at[rows(c, 128)], 1)
    sent(rfs.at[c], 2)
    sent(mx.at[c], 3)
    sent(bc.at[c], 4)
    sent(fv.at[c], 5)
    sent(wb.at[pl.ds(0, 7 * 256)], 6)
    sent(psend.at[pl.ds(0, 31)], 7)
    sent(rh.at[pl.ds(0, 31 * 32)], 8)
    sent(hp, 9)
    sent(hf.at[pl.ds(0, 7)], 10)
    sent(pf.at[pl.ds(0, 31)], 11)
    sent(hh.at[pl.ds(0, 31 * 32)], 12)
    sent(hx, 13)
    sent(fs.at[pl.ds(0, 7)], 14)
    sent(ug.at[pl.ds(0, 7 * 256)], 15)
    sent(sv, 16)
    sent(r2.at[rows(c, 128)], 17)
    out1.wait()
    out2.wait()


def per_device(right_first, right_scen, kkt_inverse, border, block_mask, factor_inverse):
    hbm = pl.BlockSpec(memory_space=pl.ANY)
    return pl.pallas_call(
        kernel,
        out_shape=(
            jax.ShapeDtypeStruct((512, 256), F32),
            jax.ShapeDtypeStruct((1, 128, 256), F32),
        ),
        in_specs=[hbm, hbm, hbm, hbm, pl.BlockSpec(memory_space=pltpu.VMEM), hbm],
        out_specs=(hbm, hbm),
        scratch_shapes=[
            pltpu.VMEM((256, 2048), BF),
            pltpu.VMEM((2, 2048, 512), BF),
            pltpu.VMEM((1024, 2048), BF),
            pltpu.VMEM((2, 256, 512), F32),
            pltpu.VMEM((256, 1024), BF),
            pltpu.VMEM((256, 1024), BF),
            pltpu.VMEM((1024, 256), BF),
            pltpu.VMEM((1024, 256), BF),
            pltpu.VMEM((2, 32, 128), F32),
            pltpu.VMEM((2, 32, 128), F32),
            pltpu.VMEM((2048, 128), BF),
            pltpu.VMEM((256, 128), BF),
            pltpu.VMEM((2048, 128), BF),
            pltpu.VMEM((32, 32, 128), BF),
            pltpu.VMEM((32, 32, 128), BF),
            pltpu.VMEM((32, 32, 128), BF),
            pltpu.VMEM((1024, 128), BF),
            pltpu.VMEM((8, 32, 128), F32),
            pltpu.VMEM((8, 32, 128), F32),
            pltpu.VMEM((8, 32, 128), F32),
            pltpu.VMEM((32, 32, 128), BF),
            pltpu.VMEM((1024, 128), BF),
            pltpu.VMEM((1024, 128), BF),
            pltpu.VMEM((8, 256, 128), BF),
            pltpu.VMEM((8, 256, 128), BF),
            pltpu.VMEM((2048, 128), BF),
            pltpu.VMEM((128, 128), F32),
            pltpu.VMEM((512, 256), F32),
            pltpu.VMEM((128, 128), F32),
            pltpu.VMEM((512, 128), BF),
            pltpu.SemaphoreType.DMA((8,)),
            pltpu.SemaphoreType.DMA((18,)),
            pltpu.SemaphoreType.DMA((18,)),
        ],
        compiler_params=pltpu.CompilerParams(
            collective_id=0, has_side_effects=True, vmem_limit_bytes=53 << 20
        ),
        cost_estimate=pl.CostEstimate(flops=3 * 10**9, bytes_accessed=8 << 20, transcendentals=0),
    )(right_first, right_scen, kkt_inverse, border, block_mask, factor_inverse)


def solution(mesh):
    in_specs = (
        P("tile", None),
        P("scen", "tile", None),
        P("scen", "tile", None),
        P("scen", None, "tile"),
        P("scen", "tile"),
        P("scen", "tile"),
    )
    out_specs = (P("tile", None), P("scen", "tile", None))
    return jax.shard_map(
        per_device, mesh=mesh, in_specs=in_specs, out_specs=out_specs, check_vma=False
    )
```

```python
import jax
import jax.numpy as jnp
from jax import lax
from jax.experimental import pallas as pl
from jax.experimental.pallas import tpu as pltpu
from jax.sharding import PartitionSpec as P

MESH = pl.DeviceIdType.MESH
BF = jnp.bfloat16
F32 = jnp.float32
SCEN, TILE, CHIPS = 32, 16, 8
HALF = 128
Y_ORDER = (4, 3, 5, 2, 6, 1, 7, 0)
Z_ORDER = (2, 1, 3, 0)
SCEN_STEPS = [(dy, dz) for dz in Z_ORDER for dy in Y_ORDER if dy or dz]
CHIP_STEPS = [(2, 1), (1, 1), (3, 1), (2, 0), (1, 0), (3, 0), (0, 1)]


def kernel(
    rf, rs, kinv, bord, mask, fac,
    o1, o2,
    kc, bc, bt, fv, fhi, flo, fthi, ftlo, rfs, mx,
    ra, wb, pf, psend, cr, rh, hp, dr, hf, er, hh, hm, fs, fr, ug, sv, o1v, o2v, hx,
    loc, ssem, rsem,
):
    s = lax.axis_index("scen")
    t = lax.axis_index("tile")
    q, c = t // 2, t % 2
    x, zl = q // 2, q % 2
    y, zh = s // 4, s % 4
    oc = 1 - c
    sib = (s, q * 2 + oc)

    def chip(dx, dz):
        return ((x + dx) % 4) * 2 + (zl + dz) % 2

    chips = [chip(dx, dz) for dx, dz in CHIP_STEPS]
    scens = [((y + dy) % 8) * 4 + (zh + dz) % 4 for dy, dz in SCEN_STEPS]

    def remote(src, dst, n, dev):
        pltpu.make_async_remote_copy(
            src_ref=src, dst_ref=dst, send_sem=ssem.at[n], recv_sem=rsem.at[n],
            device_id=dev, device_id_type=MESH,
        ).start()

    def arrived(ref, n):
        pltpu.make_async_copy(ref, ref, rsem.at[n]).wait()

    def sent(ref, n):
        pltpu.make_async_copy(ref, ref, ssem.at[n]).wait()

    def rows(i, n):
        return pl.ds(pl.multiple_of(i * n, n), n)

    own = [
        pltpu.make_async_copy(kinv.at[0], kc.at[rows(c, 128)], loc.at[0]),
        pltpu.make_async_copy(bord.at[0], bc.at[c], loc.at[1]),
        pltpu.make_async_copy(fac, fv.at[c], loc.at[2]),
        pltpu.make_async_copy(rf.at[rows(s % 16, 32), rows(c, 128)], rfs.at[c], loc.at[3]),
        pltpu.make_async_copy(rs.at[0, :, rows(c, 128)], ra.at[rows(t, 128)], loc.at[4]),
    ]
    for cp in own:
        cp.start()

    barrier = pltpu.get_barrier_semaphore()
    for p in chips:
        for cc in range(2):
            pl.semaphore_signal(barrier, inc=1, device_id=(s, p * 2 + cc), device_id_type=MESH)
    pl.semaphore_signal(barrier, inc=1, device_id=sib, device_id_type=MESH)
    for p in scens:
        pl.semaphore_signal(barrier, inc=1, device_id=(p, t), device_id_type=MESH)
    pl.semaphore_wait(barrier, TILE - 1 + SCEN - 1)

    for cc in (1, 0):
        for p in chips:
            remote(rs.at[0, :, rows(cc, 128)], ra.at[rows(t, 128)], 0, (s, p * 2 + cc))
    remote(rs.at[0, :, rows(oc, 128)], ra.at[rows(t, 128)], 0, sib)
    remote(kinv.at[0], kc.at[rows(c, 128)], 1, sib)
    remote(rf.at[rows(s % 16, 32), rows(oc, 128)], rfs.at[c], 2, sib)
    for b in range(4):
        mx[c, pl.ds(b * 8, 8)] = jnp.broadcast_to(mask[0:1, b : b + 1].astype(F32), (8, 128))
    remote(mx.at[c], mx.at[c], 3, sib)
    remote(bord.at[0], bc.at[c], 4, sib)
    remote(fac, fv.at[c], 5, sib)

    own[0].wait()
    own[4].wait()
    arrived(kc.at[rows(oc, 128)], 1)
    arrived(ra.at[pl.ds(0, 15 * 128)], 0)
    for i in range(2):
        r = pl.ds(i * 128, 128)
        w = jnp.dot(kc[r], ra[...], preferred_element_type=F32)
        wb[pl.ds(pl.multiple_of(q * 256 + i * 128, 128), 128)] = w.astype(BF)
    for p in chips:
        remote(wb.at[rows(q, 256)], wb.at[rows(q, 256)], 6, (s, p * 2 + c))

    own[1].wait()
    arrived(bc.at[oc], 4)
    arrived(mx.at[oc], 3)

    @pl.loop(0, 8)
    def _(i):
        for cc in range(2):
            for j in range(2):
                blk = bc[cc, rows(i, 256), pl.ds(j * 256, 256)]
                bt[pl.ds(cc * 512 + j * 256, 256), rows(i, 256)] = blk.T

    arrived(wb.at[pl.ds(0, 7 * 256)], 6)
    for k in range(4):
        r = (s // 8 + k) % 4
        p = jnp.dot(bt[rows(r, 256)], wb[...], preferred_element_type=F32)
        for j in range(2):
            keep = mx[r // 2, pl.ds(pl.multiple_of((r % 2) * 16 + j * 8, 8), 1)]
            v = jnp.where(keep > 0.5, p[j * 128 : (j + 1) * 128], 0.0)
            psend[pl.ds(r * 8 + j * 4, 4)] = v.astype(BF).reshape(4, 32, 128)
        for j in range(8):
            d = r * 8 + (s % 8 + j) % 8

            @pl.when(d != s)
            def _():
                remote(psend.at[d], cr.at[s], 7, (d, t))

    own[2].wait()
    arrived(fv.at[oc], 5)
    for cc in range(2):
        for j in range(2):
            v = fv[cc, :, pl.ds(j * 256, 256)]
            hi = v.astype(BF)
            lo = (v - hi.astype(F32)).astype(BF)
            at = pl.ds(cc * 512 + j * 256, 256)
            fhi[:, at] = hi
            flo[:, at] = lo
            fthi[at] = hi.T
            ftlo[at] = lo.T
    own[3].wait()
    arrived(rfs.at[oc], 2)
    cr[s] = psend[s]
    arrived(psend.at[pl.ds(0, 31)], 7)
    total = cr[0].astype(F32)
    for i in range(1, SCEN):
        total += cr[i].astype(F32)
    rh[rows(s, 32)] = (rfs[s // 16] - total).astype(BF)
    for p in scens:
        remote(rh.at[rows(s, 32)], rh.at[rows(s, 32)], 8, (p, t))
    arrived(rh.at[pl.ds(0, 31 * 32)], 8)

    for i in range(2):
        r = pl.ds(i * 128, 128)
        h = jnp.dot(fhi[r], rh[...], preferred_element_type=F32)
        h += jnp.dot(flo[r], rh[...], preferred_element_type=F32)
        hp[pl.ds(i * 4, 4)] = h.reshape(4, 32, 128)
    for p in chips:
        remote(hp.at[p], dr.at[q], 9, (s, p * 2 + c))
    dr[q] = hp[q]
    arrived(dr.at[pl.ds(0, 7)], 9)
    total = dr[0]
    for i in range(1, CHIPS):
        total += dr[i]
    hf[q] = total
    for p in chips:
        remote(hf.at[q], hf.at[q], 10, (s, p * 2 + c))
    arrived(hf.at[pl.ds(0, 7)], 10)

    half = hf[...].reshape(256, HALF)
    hhi = half.astype(BF)
    hlo = (half - hhi.astype(F32)).astype(BF)
    for k in range(4):
        r = (s // 8 + k) % 4
        v = jnp.dot(fthi[rows(r, 256)], hhi, preferred_element_type=F32)
        v += jnp.dot(fthi[rows(r, 256)], hlo, preferred_element_type=F32)
        v += jnp.dot(ftlo[rows(r, 256)], hhi, preferred_element_type=F32)
        pf[pl.ds(r * 8, 8)] = v.astype(BF).reshape(8, 32, 128)
        for j in range(8):
            d = r * 8 + (s % 8 + j) % 8

            @pl.when(d != s)
            def _():
                remote(pf.at[d], er.at[s], 11, (d, t))

    er[s] = pf[s]
    arrived(pf.at[pl.ds(0, 31)], 11)
    total = er[0].astype(F32)
    for i in range(1, SCEN):
        total += er[i].astype(F32)
    hh[rows(s, 32)] = total.astype(BF)
    for p in scens:
        remote(hh.at[rows(s, 32)], hh.at[rows(s, 32)], 12, (p, t))
    arrived(hh.at[pl.ds(0, 31 * 32)], 12)

    remote(hh.at[rows(oc, 512)], hx.at[pl.ds(0, 512)], 13, sib)
    for b in range(8):
        keep = mx[b // 4, pl.ds((b % 4) * 8, 1)]
        v = hh[pl.ds(b * 128, 128)].astype(F32)
        hm[pl.ds(b * 128, 128)] = jnp.where(keep > 0.5, v, 0.0).astype(BF)
    for p in [*chips, q]:
        at = rows(p, 256)
        v = jnp.dot(bc[0, at], hm[pl.ds(0, 512)], preferred_element_type=F32)
        v += jnp.dot(bc[1, at], hm[pl.ds(512, 512)], preferred_element_type=F32)
        fs[p] = v.astype(BF)
        if p is not q:
            remote(fs.at[p], fr.at[q], 14, (s, p * 2 + c))
    fr[q] = fs[q]

    arrived(hx, 13)
    o1v[:, rows(c, 128)] = hh[rows(c, 512)].astype(F32)
    o1v[:, rows(oc, 128)] = hx[...].astype(F32)
    out1 = pltpu.make_async_copy(o1v, o1, loc.at[5])
    out1.start()

    arrived(fs.at[pl.ds(0, 7)], 14)
    total = fr[0].astype(F32)
    for i in range(1, CHIPS):
        total += fr[i].astype(F32)
    ug[rows(q, 256)] = (ra[rows(q, 256)].astype(F32) - total).astype(BF)
    for p in chips:
        remote(ug.at[rows(q, 256)], ug.at[rows(q, 256)], 15, (s, p * 2 + c))
    arrived(ug.at[pl.ds(0, 7 * 256)], 15)
    sv[...] = jnp.dot(kc[rows(oc, 128)], ug[...], preferred_element_type=F32)
    remote(sv, o2.at[0, :, rows(c, 128)], 16, sib)
    o2v[...] = jnp.dot(kc[rows(c, 128)], ug[...], preferred_element_type=F32)
    out2 = pltpu.make_async_copy(o2v, o2.at[0, :, rows(c, 128)], loc.at[6])
    out2.start()
    arrived(sv, 16)

    sent(ra.at[pl.ds(0, 15 * 128)], 0)
    sent(kc.at[rows(c, 128)], 1)
    sent(rfs.at[c], 2)
    sent(mx.at[c], 3)
    sent(bc.at[c], 4)
    sent(fv.at[c], 5)
    sent(wb.at[pl.ds(0, 7 * 256)], 6)
    sent(psend.at[pl.ds(0, 31)], 7)
    sent(rh.at[pl.ds(0, 31 * 32)], 8)
    sent(hp.at[pl.ds(0, 7)], 9)
    sent(hf.at[pl.ds(0, 7)], 10)
    sent(pf.at[pl.ds(0, 31)], 11)
    sent(hh.at[pl.ds(0, 31 * 32)], 12)
    sent(hx, 13)
    sent(fs.at[pl.ds(0, 7)], 14)
    sent(ug.at[pl.ds(0, 7 * 256)], 15)
    sent(sv, 16)
    out1.wait()
    out2.wait()


def per_device(right_first, right_scen, kkt_inverse, border, block_mask, factor_inverse):
    hbm = pl.BlockSpec(memory_space=pl.ANY)
    return pl.pallas_call(
        kernel,
        out_shape=(
            jax.ShapeDtypeStruct((512, 256), F32),
            jax.ShapeDtypeStruct((1, 128, 256), F32),
        ),
        in_specs=[hbm, hbm, hbm, hbm, pl.BlockSpec(memory_space=pltpu.VMEM), hbm],
        out_specs=(hbm, hbm),
        scratch_shapes=[
            pltpu.VMEM((256, 2048), BF),
            pltpu.VMEM((2, 2048, 512), BF),
            pltpu.VMEM((1024, 2048), BF),
            pltpu.VMEM((2, 256, 512), F32),
            pltpu.VMEM((256, 1024), BF),
            pltpu.VMEM((256, 1024), BF),
            pltpu.VMEM((1024, 256), BF),
            pltpu.VMEM((1024, 256), BF),
            pltpu.VMEM((2, 32, 128), F32),
            pltpu.VMEM((2, 32, 128), F32),
            pltpu.VMEM((2048, 128), BF),
            pltpu.VMEM((2048, 128), BF),
            pltpu.VMEM((32, 32, 128), BF),
            pltpu.VMEM((32, 32, 128), BF),
            pltpu.VMEM((32, 32, 128), BF),
            pltpu.VMEM((1024, 128), BF),
            pltpu.VMEM((8, 32, 128), F32),
            pltpu.VMEM((8, 32, 128), F32),
            pltpu.VMEM((8, 32, 128), F32),
            pltpu.VMEM((32, 32, 128), BF),
            pltpu.VMEM((1024, 128), BF),
            pltpu.VMEM((1024, 128), BF),
            pltpu.VMEM((8, 256, 128), BF),
            pltpu.VMEM((8, 256, 128), BF),
            pltpu.VMEM((2048, 128), BF),
            pltpu.VMEM((128, 128), F32),
            pltpu.VMEM((512, 256), F32),
            pltpu.VMEM((128, 128), F32),
            pltpu.VMEM((512, 128), BF),
            pltpu.SemaphoreType.DMA((7,)),
            pltpu.SemaphoreType.DMA((17,)),
            pltpu.SemaphoreType.DMA((17,)),
        ],
        compiler_params=pltpu.CompilerParams(
            collective_id=0, has_side_effects=True, vmem_limit_bytes=53 << 20
        ),
        cost_estimate=pl.CostEstimate(flops=3 * 10**9, bytes_accessed=8 << 20, transcendentals=0),
    )(right_first, right_scen, kkt_inverse, border, block_mask, factor_inverse)


def solution(mesh):
    in_specs = (
        P("tile", None),
        P("scen", "tile", None),
        P("scen", "tile", None),
        P("scen", None, "tile"),
        P("scen", "tile"),
        P("scen", "tile"),
    )
    out_specs = (P("tile", None), P("scen", "tile", None))
    return jax.shard_map(
        per_device, mesh=mesh, in_specs=in_specs, out_specs=out_specs, check_vma=False
    )
```

```python
import jax
import jax.numpy as jnp
from jax import lax
from jax.experimental import pallas as pl
from jax.experimental.pallas import tpu as pltpu
from jax.sharding import PartitionSpec as P

MESH = pl.DeviceIdType.MESH
BF = jnp.bfloat16
F32 = jnp.float32
SCEN, TILE, CHIPS = 32, 16, 8
HALF = 128
Y_ORDER = (4, 3, 5, 2, 6, 1, 7, 0)
Z_ORDER = (2, 1, 3, 0)
SCEN_STEPS = [(dy, dz) for dz in Z_ORDER for dy in Y_ORDER if dy or dz]
CHIP_STEPS = [(2, 1), (1, 1), (3, 1), (2, 0), (1, 0), (3, 0), (0, 1)]


def kernel(
    rf, rs, kinv, bord, mask, fac,
    o1, o2,
    kc, bc, bt, fv, fhi, flo, fthi, ftlo, rfs, mx,
    ra, wb, pf, psend, cr, rh, hp, dr, hf, er, hh, hm, fs, fr, ug, sv, o1v, o2v, hx,
    loc, ssem, rsem,
):
    s = lax.axis_index("scen")
    t = lax.axis_index("tile")
    q, c = t // 2, t % 2
    x, zl = q // 2, q % 2
    y, zh = s // 4, s % 4
    oc = 1 - c
    sib = (s, q * 2 + oc)

    def chip(dx, dz):
        return ((x + dx) % 4) * 2 + (zl + dz) % 2

    chips = [chip(dx, dz) for dx, dz in CHIP_STEPS]
    scens = [((y + dy) % 8) * 4 + (zh + dz) % 4 for dy, dz in SCEN_STEPS]

    def remote(src, dst, n, dev):
        pltpu.make_async_remote_copy(
            src_ref=src, dst_ref=dst, send_sem=ssem.at[n], recv_sem=rsem.at[n],
            device_id=dev, device_id_type=MESH,
        ).start()

    def arrived(ref, n):
        pltpu.make_async_copy(ref, ref, rsem.at[n]).wait()

    def sent(ref, n):
        pltpu.make_async_copy(ref, ref, ssem.at[n]).wait()

    def rows(i, n):
        return pl.ds(pl.multiple_of(i * n, n), n)

    own = [
        pltpu.make_async_copy(kinv.at[0], kc.at[rows(c, 128)], loc.at[0]),
        pltpu.make_async_copy(bord.at[0], bc.at[c], loc.at[1]),
        pltpu.make_async_copy(fac, fv.at[c], loc.at[2]),
        pltpu.make_async_copy(rf.at[rows(s % 16, 32), rows(c, 128)], rfs.at[c], loc.at[3]),
        pltpu.make_async_copy(rs.at[0, :, rows(c, 128)], ra.at[rows(t, 128)], loc.at[4]),
    ]
    for cp in own:
        cp.start()

    barrier = pltpu.get_barrier_semaphore()
    for p in chips:
        for cc in range(2):
            pl.semaphore_signal(barrier, inc=1, device_id=(s, p * 2 + cc), device_id_type=MESH)
    pl.semaphore_signal(barrier, inc=1, device_id=sib, device_id_type=MESH)
    for p in scens:
        pl.semaphore_signal(barrier, inc=1, device_id=(p, t), device_id_type=MESH)
    pl.semaphore_wait(barrier, TILE - 1 + SCEN - 1)

    for cc in (1, 0):
        for p in chips:
            remote(rs.at[0, :, rows(cc, 128)], ra.at[rows(t, 128)], 0, (s, p * 2 + cc))
    remote(rs.at[0, :, rows(oc, 128)], ra.at[rows(t, 128)], 0, sib)
    remote(kinv.at[0], kc.at[rows(c, 128)], 1, sib)
    remote(rf.at[rows(s % 16, 32), rows(oc, 128)], rfs.at[c], 2, sib)
    for b in range(4):
        mx[c, pl.ds(b * 8, 8)] = jnp.broadcast_to(mask[0:1, b : b + 1].astype(F32), (8, 128))
    remote(mx.at[c], mx.at[c], 3, sib)
    remote(bord.at[0], bc.at[c], 4, sib)
    remote(fac, fv.at[c], 5, sib)

    own[0].wait()
    own[4].wait()
    arrived(kc.at[rows(oc, 128)], 1)
    arrived(ra.at[pl.ds(0, 15 * 128)], 0)
    for i in range(2):
        r = pl.ds(i * 128, 128)
        w = jnp.dot(kc[r], ra[...], preferred_element_type=F32)
        wb[pl.ds(pl.multiple_of(q * 256 + i * 128, 128), 128)] = w.astype(BF)
    for p in chips:
        remote(wb.at[rows(q, 256)], wb.at[rows(q, 256)], 6, (s, p * 2 + c))

    own[1].wait()
    arrived(bc.at[oc], 4)
    arrived(mx.at[oc], 3)

    @pl.loop(0, 8)
    def _(i):
        for cc in range(2):
            for j in range(2):
                blk = bc[cc, rows(i, 256), pl.ds(j * 256, 256)]
                bt[pl.ds(cc * 512 + j * 256, 256), rows(i, 256)] = blk.T

    arrived(wb.at[pl.ds(0, 7 * 256)], 6)
    for k in (2, 1, 3, 0):
        r = (s // 8 + k) % 4
        p = jnp.dot(bt[rows(r, 256)], wb[...], preferred_element_type=F32)
        for j in range(2):
            keep = mx[r // 2, pl.ds(pl.multiple_of((r % 2) * 16 + j * 8, 8), 1)]
            v = jnp.where(keep > 0.5, p[j * 128 : (j + 1) * 128], 0.0)
            psend[pl.ds(r * 8 + j * 4, 4)] = v.astype(BF).reshape(4, 32, 128)
        for j in (2, 6, 1, 5, 3, 7, 4, 0):
            d = r * 8 + (s % 8 + j) % 8

            @pl.when(d != s)
            def _():
                remote(psend.at[d], cr.at[s], 7, (d, t))

    own[2].wait()
    arrived(fv.at[oc], 5)
    for cc in range(2):
        for j in range(2):
            v = fv[cc, :, pl.ds(j * 256, 256)]
            hi = v.astype(BF)
            lo = (v - hi.astype(F32)).astype(BF)
            at = pl.ds(cc * 512 + j * 256, 256)
            fhi[:, at] = hi
            flo[:, at] = lo
            fthi[at] = hi.T
            ftlo[at] = lo.T
    own[3].wait()
    arrived(rfs.at[oc], 2)
    cr[s] = psend[s]
    arrived(psend.at[pl.ds(0, 31)], 7)
    total = cr[0].astype(F32)
    for i in range(1, SCEN):
        total += cr[i].astype(F32)
    rh[rows(s, 32)] = (rfs[s // 16] - total).astype(BF)
    for p in scens:
        remote(rh.at[rows(s, 32)], rh.at[rows(s, 32)], 8, (p, t))
    arrived(rh.at[pl.ds(0, 31 * 32)], 8)

    for i in range(2):
        r = pl.ds(i * 128, 128)
        h = jnp.dot(fhi[r], rh[...], preferred_element_type=F32)
        h += jnp.dot(flo[r], rh[...], preferred_element_type=F32)
        hp[pl.ds(i * 4, 4)] = h.reshape(4, 32, 128)
    for p in chips:
        remote(hp.at[p], dr.at[q], 9, (s, p * 2 + c))
    dr[q] = hp[q]
    arrived(dr.at[pl.ds(0, 7)], 9)
    total = dr[0]
    for i in range(1, CHIPS):
        total += dr[i]
    hf[q] = total
    for p in chips:
        remote(hf.at[q], hf.at[q], 10, (s, p * 2 + c))
    arrived(hf.at[pl.ds(0, 7)], 10)

    half = hf[...].reshape(256, HALF)
    hhi = half.astype(BF)
    hlo = (half - hhi.astype(F32)).astype(BF)
    for k in (2, 1, 3, 0):
        r = (s // 8 + k) % 4
        v = jnp.dot(fthi[rows(r, 256)], hhi, preferred_element_type=F32)
        v += jnp.dot(fthi[rows(r, 256)], hlo, preferred_element_type=F32)
        v += jnp.dot(ftlo[rows(r, 256)], hhi, preferred_element_type=F32)
        pf[pl.ds(r * 8, 8)] = v.astype(BF).reshape(8, 32, 128)
        for j in (2, 6, 1, 5, 3, 7, 4, 0):
            d = r * 8 + (s % 8 + j) % 8

            @pl.when(d != s)
            def _():
                remote(pf.at[d], er.at[s], 11, (d, t))

    er[s] = pf[s]
    arrived(pf.at[pl.ds(0, 31)], 11)
    total = er[0].astype(F32)
    for i in range(1, SCEN):
        total += er[i].astype(F32)
    hh[rows(s, 32)] = total.astype(BF)
    for p in scens:
        remote(hh.at[rows(s, 32)], hh.at[rows(s, 32)], 12, (p, t))
    arrived(hh.at[pl.ds(0, 31 * 32)], 12)

    remote(hh.at[rows(oc, 512)], hx.at[pl.ds(0, 512)], 13, sib)
    for b in range(8):
        keep = mx[b // 4, pl.ds((b % 4) * 8, 1)]
        v = hh[pl.ds(b * 128, 128)].astype(F32)
        hm[pl.ds(b * 128, 128)] = jnp.where(keep > 0.5, v, 0.0).astype(BF)
    for p in [*chips, q]:
        at = rows(p, 256)
        v = jnp.dot(bc[0, at], hm[pl.ds(0, 512)], preferred_element_type=F32)
        v += jnp.dot(bc[1, at], hm[pl.ds(512, 512)], preferred_element_type=F32)
        fs[p] = v.astype(BF)
        if p is not q:
            remote(fs.at[p], fr.at[q], 14, (s, p * 2 + c))
    fr[q] = fs[q]

    arrived(hx, 13)
    o1v[:, rows(c, 128)] = hh[rows(c, 512)].astype(F32)
    o1v[:, rows(oc, 128)] = hx[...].astype(F32)
    out1 = pltpu.make_async_copy(o1v, o1, loc.at[5])
    out1.start()

    arrived(fs.at[pl.ds(0, 7)], 14)
    total = fr[0].astype(F32)
    for i in range(1, CHIPS):
        total += fr[i].astype(F32)
    ug[rows(q, 256)] = (ra[rows(q, 256)].astype(F32) - total).astype(BF)
    for p in chips:
        remote(ug.at[rows(q, 256)], ug.at[rows(q, 256)], 15, (s, p * 2 + c))
    arrived(ug.at[pl.ds(0, 7 * 256)], 15)
    sv[...] = jnp.dot(kc[rows(oc, 128)], ug[...], preferred_element_type=F32)
    remote(sv, o2.at[0, :, rows(c, 128)], 16, sib)
    o2v[...] = jnp.dot(kc[rows(c, 128)], ug[...], preferred_element_type=F32)
    out2 = pltpu.make_async_copy(o2v, o2.at[0, :, rows(c, 128)], loc.at[6])
    out2.start()
    arrived(sv, 16)

    sent(ra.at[pl.ds(0, 15 * 128)], 0)
    sent(kc.at[rows(c, 128)], 1)
    sent(rfs.at[c], 2)
    sent(mx.at[c], 3)
    sent(bc.at[c], 4)
    sent(fv.at[c], 5)
    sent(wb.at[pl.ds(0, 7 * 256)], 6)
    sent(psend.at[pl.ds(0, 31)], 7)
    sent(rh.at[pl.ds(0, 31 * 32)], 8)
    sent(hp.at[pl.ds(0, 7)], 9)
    sent(hf.at[pl.ds(0, 7)], 10)
    sent(pf.at[pl.ds(0, 31)], 11)
    sent(hh.at[pl.ds(0, 31 * 32)], 12)
    sent(hx, 13)
    sent(fs.at[pl.ds(0, 7)], 14)
    sent(ug.at[pl.ds(0, 7 * 256)], 15)
    sent(sv, 16)
    out1.wait()
    out2.wait()


def per_device(right_first, right_scen, kkt_inverse, border, block_mask, factor_inverse):
    hbm = pl.BlockSpec(memory_space=pl.ANY)
    return pl.pallas_call(
        kernel,
        out_shape=(
            jax.ShapeDtypeStruct((512, 256), F32),
            jax.ShapeDtypeStruct((1, 128, 256), F32),
        ),
        in_specs=[hbm, hbm, hbm, hbm, pl.BlockSpec(memory_space=pltpu.VMEM), hbm],
        out_specs=(hbm, hbm),
        scratch_shapes=[
            pltpu.VMEM((256, 2048), BF),
            pltpu.VMEM((2, 2048, 512), BF),
            pltpu.VMEM((1024, 2048), BF),
            pltpu.VMEM((2, 256, 512), F32),
            pltpu.VMEM((256, 1024), BF),
            pltpu.VMEM((256, 1024), BF),
            pltpu.VMEM((1024, 256), BF),
            pltpu.VMEM((1024, 256), BF),
            pltpu.VMEM((2, 32, 128), F32),
            pltpu.VMEM((2, 32, 128), F32),
            pltpu.VMEM((2048, 128), BF),
            pltpu.VMEM((2048, 128), BF),
            pltpu.VMEM((32, 32, 128), BF),
            pltpu.VMEM((32, 32, 128), BF),
            pltpu.VMEM((32, 32, 128), BF),
            pltpu.VMEM((1024, 128), BF),
            pltpu.VMEM((8, 32, 128), F32),
            pltpu.VMEM((8, 32, 128), F32),
            pltpu.VMEM((8, 32, 128), F32),
            pltpu.VMEM((32, 32, 128), BF),
            pltpu.VMEM((1024, 128), BF),
            pltpu.VMEM((1024, 128), BF),
            pltpu.VMEM((8, 256, 128), BF),
            pltpu.VMEM((8, 256, 128), BF),
            pltpu.VMEM((2048, 128), BF),
            pltpu.VMEM((128, 128), F32),
            pltpu.VMEM((512, 256), F32),
            pltpu.VMEM((128, 128), F32),
            pltpu.VMEM((512, 128), BF),
            pltpu.SemaphoreType.DMA((7,)),
            pltpu.SemaphoreType.DMA((17,)),
            pltpu.SemaphoreType.DMA((17,)),
        ],
        compiler_params=pltpu.CompilerParams(
            collective_id=0, has_side_effects=True, vmem_limit_bytes=53 << 20
        ),
        cost_estimate=pl.CostEstimate(flops=3 * 10**9, bytes_accessed=8 << 20, transcendentals=0),
    )(right_first, right_scen, kkt_inverse, border, block_mask, factor_inverse)


def solution(mesh):
    in_specs = (
        P("tile", None),
        P("scen", "tile", None),
        P("scen", "tile", None),
        P("scen", None, "tile"),
        P("scen", "tile"),
        P("scen", "tile"),
    )
    out_specs = (P("tile", None), P("scen", "tile", None))
    return jax.shard_map(
        per_device, mesh=mesh, in_specs=in_specs, out_specs=out_specs, check_vma=False
    )
```
